32 devices in a mesh: row: 8 (over z, y), col: 4 (over x, core).
Axes of the slice: x: 2, y: 2, z: 4, core: 2. Of those that a mesh axis runs over, the one named last changes fastest.
Arguments:
- table: float32 [4, 256, 256], P('col', 'row'), may hold values from -4 to 4
- marginals: int32 [1024], replicated, may hold values from 64 to 4095
- visits: int32 [8, 4, 16], P('row', 'col'), may hold values from 0 to 3
- counts: int32 [8, 4, 16, 256, 256], P('row', 'col'), may hold values from 0 to 16, as said below
Outputs:
- gradient: float32 [4, 256, 256], P('col')
The draws below stay inside these ranges and needn't reach their ends.
Inputs may be any that keep to these rules, and one draw needn't show every extreme that they name: `counts`: about half of the cells of every tile are zero.
All inputs are finite; a program needn't handle non-finite values.
Results may differ from the reference program's by a relative error of at most 0.0031.
Values may be sent and summed in bfloat16 or wider, within the bound.
No kernel may reach another device: no remote copies, remote signals or barrier semaphores. Data moves between devices by JAX's collectives and lax.ppermute only.
A program may use at most 128 MiB of HBM per device.

```python
import jax
import jax.numpy as jnp
from jax import lax

D = 256
B = 256
K = 16
NBLK = 4
VOCAB = 1024
N_ROW = 8
N_COL = 4


def draw_counts(key, part):
    shape_all = (N_ROW, N_COL, K, B, B)
    live_key, value_key = jax.random.split(jax.random.fold_in(key, 11))
    live = jax.random.randint(live_key, shape_all, 0, 2)
    values = jax.random.randint(value_key, shape_all, 1, 17)
    return jnp.where(live == 1, values, 0).astype(jnp.int32)


def with_ends(values, stream_key, smallest, top_value):
    index_at = [jax.random.randint(jax.random.fold_in(stream_key, axis), (), 0, length) for axis, length in enumerate(values.shape)]
    longest = values.shape.index(max(values.shape))
    beside = index_at[:longest] + [(index_at[longest] + 1) % values.shape[longest]] + index_at[longest + 1:]
    return values.at[tuple(index_at)].set(smallest).at[tuple(beside)].set(top_value)


def shard_levels(key, shape, pieces, smallest, top_value):
    factor_of, own = 1.0, jax.random.fold_in(key, 6)
    for dim, shards_of in pieces:
        draws = jnp.exp(jax.random.uniform(jax.random.fold_in(own, dim), (shards_of,), jnp.float32, smallest / len(pieces), top_value / len(pieces)))
        factor_of = factor_of * jnp.repeat(draws, shape[dim] // shards_of).reshape([-1 if axis == dim else 1 for axis in range(len(shape))])
    return factor_of


def bell_draw(key, extent, deviation, most, shards=(), held_as=jnp.bfloat16):
    loudness = shard_levels(key, extent, shards, -0.22, 0.18) if shards else 1.0
    entries = jax.random.normal(key, extent, jnp.float32) * deviation * loudness
    return jnp.minimum(jnp.maximum(entries, -most), most).astype(held_as)


def setup_inputs(seed: int = 0) -> dict:
    key_list = jax.random.split(jax.random.key(seed), 5)
    table = bell_draw(key_list[0], (NBLK, B, D), (D ** -0.25), 4.0, ((0, 4), (1, 8)), jnp.float32)
    marginals = with_ends(jax.random.randint(key_list[1], (VOCAB,), 64, 4096), jax.random.fold_in(key_list[1], 1), 64, 4095).astype(jnp.int32)
    visits = with_ends(jax.random.randint(key_list[2], (N_ROW, N_COL, K), 0, N_COL), jax.random.fold_in(key_list[2], 1), 0, N_COL - 1).astype(jnp.int32)
    counts = draw_counts(jax.random.fold_in(key_list[4], 71), 0)
    return {"table": table, "marginals": marginals, "visits": visits, "counts": counts}


LOSS_SCALE = 0.0625

def tile_terms(row_vectors, col_vectors, count_tile, log_rows, log_cols, log_total):
    logits = lax.dot_general(row_vectors, col_vectors, (((1,), (1,)), ((), ())), preferred_element_type=jnp.float32)
    count_vals = count_tile.astype(jnp.float32)
    baseline = log_total - log_rows[:, None] - log_cols[None, :]
    margin = logits - baseline
    fitted = (0.1 + 0.25 * jnp.sqrt(count_vals)) * (margin - jnp.log(jnp.maximum(count_vals, 1.0)))
    soft_hinge = jax.nn.sigmoid(margin)
    grad_logits = (jnp.where(count_vals > 0, fitted, soft_hinge) * LOSS_SCALE).astype(jnp.bfloat16)
    row_term = jnp.dot(grad_logits, col_vectors, preferred_element_type=jnp.float32)
    col_term = lax.dot_general(grad_logits, row_vectors, (((0,), (0,)), ((), ())), preferred_element_type=jnp.float32)
    return (row_term, col_term)

def reference(table, marginals, visits, counts):
    table_bf = table.astype(jnp.bfloat16)
    log_marg = jnp.log(marginals.astype(jnp.float32)).reshape(N_COL, B)
    log_total = jnp.log(jnp.sum(marginals).astype(jnp.float32))
    flat_visits = visits.reshape(N_ROW * N_COL, K)
    flat_counts = counts.reshape(N_ROW * N_COL, K, B, B)

    def device_step(running, scanned):
        device_id, visited, count_tiles = scanned
        own_block = device_id // N_COL % N_COL
        row_vectors = table_bf[own_block]
        log_rows = log_marg[own_block]
        partial_value = jnp.zeros((N_COL, B, D), jnp.float32)
        row_sum = jnp.zeros((B, D), jnp.float32)
        for k in range(K):
            visit_id = visited[k]
            row_term, col_term = tile_terms(row_vectors, table_bf[visit_id], count_tiles[k], log_rows, log_marg[visit_id], log_total)
            row_sum = row_sum + row_term
            partial_value = partial_value.at[visit_id].add(col_term)
        partial_value = partial_value.at[own_block].add(row_sum)
        return (running + partial_value, None)
    device_ids = jnp.arange(N_ROW * N_COL, dtype=jnp.int32)
    gradient, unused = lax.scan(device_step, jnp.zeros((N_COL, B, D), jnp.float32), (device_ids, flat_visits, flat_counts))
    return gradient
```

```python
import functools
import math

import jax
import jax.numpy as jnp
from jax import lax
from jax.experimental import pallas as pl
from jax.experimental.pallas import tpu as pltpu
from jax.sharding import Mesh, PartitionSpec as P

LOSS_SCALE = 0.0625
ROW = ("far", "near")
COL = ("chip", "core")
NT = (((1,), (1,)), ((), ()))
TN = (((0,), (0,)), ((), ()))
VMEM = pl.BlockSpec(memory_space=pltpu.VMEM)


MIB = 1024 * 1024


def count_kernel(tiles, visits_ref, counts_ref, roots_ref, logs_ref, live_ref, tiles_ref, visits, held, visits_sem, sems):
    size = counts_ref.shape[1]
    step = 32

    def fetch(k):
        return pltpu.make_async_copy(counts_ref.at[k], held.at[k], sems.at[k])

    fetch_visits = pltpu.make_async_copy(visits_ref, visits, visits_sem)
    fetch_visits.start()
    for k in range(tiles):
        fetch(k).start()
    for ref in (roots_ref, logs_ref, live_ref):
        ref[...] = jnp.zeros_like(ref)
    fetch_visits.wait()
    for v in range(tiles_ref.shape[0]):
        visited = 0
        for k in range(tiles):
            visited += (visits[0, 0, k] == v).astype(jnp.int32)
        tiles_ref[v : v + 1] = jnp.full((1, tiles_ref.shape[1]), visited.astype(jnp.float32))

    def add_tile(k, carry):
        fetch(k).wait()
        v = visits[0, 0, k]
        for first in range(0, size, step):
            rows = pl.ds(first, step)
            n = held[k, rows].astype(jnp.float32)
            clipped = jnp.maximum(n, 1.0)
            root = n * lax.rsqrt(clipped)
            roots_ref[v, rows] += root
            logs_ref[v, rows] += (root + 0.4) * jnp.log(clipped)
            live_ref[v, rows] += jnp.minimum(n, 1.0).astype(jnp.bfloat16)
        return carry

    lax.fori_loop(0, tiles, add_tile, 0)


def sum_counts(blocks, visits, counts):
    tiles, size = counts.shape[:2]
    hbm = pl.BlockSpec(memory_space=pltpu.HBM)
    return pl.pallas_call(
        functools.partial(count_kernel, tiles),
        out_shape=[
            jax.ShapeDtypeStruct((blocks, size, size), jnp.float32),
            jax.ShapeDtypeStruct((blocks, size, size), jnp.float32),
            jax.ShapeDtypeStruct((blocks, size, size), jnp.bfloat16),
            jax.ShapeDtypeStruct((blocks, size), jnp.float32),
        ],
        in_specs=[hbm, hbm],
        out_specs=[VMEM] * 4,
        scratch_shapes=[
            pltpu.SMEM(visits.shape, jnp.int32),
            pltpu.VMEM(counts.shape, jnp.int32),
            pltpu.SemaphoreType.DMA,
            pltpu.SemaphoreType.DMA((tiles,)),
        ],
        compiler_params=pltpu.CompilerParams(vmem_limit_bytes=(12 + 2 * blocks) * MIB),
        cost_estimate=pl.CostEstimate(
            flops=10 * counts.size, bytes_accessed=4 * counts.size, transcendentals=2 * counts.size
        ),
        name="sum_counts",
    )(pltpu.with_memory_space_constraint(visits, pltpu.HBM), pltpu.with_memory_space_constraint(counts, pltpu.HBM))


def stack_kernel(places, *refs):
    *parts, out_ref = refs
    for j, part in zip(places, parts):
        out_ref[j] = part[...].astype(out_ref.dtype)


def stack(parts):
    places = [0, *range(2, len(parts)), 1]
    return pl.pallas_call(
        functools.partial(stack_kernel, places),
        out_shape=jax.ShapeDtypeStruct((len(parts), *parts[0].shape), jnp.bfloat16),
        in_specs=[VMEM] * len(parts),
        out_specs=VMEM,
        compiler_params=pltpu.CompilerParams(vmem_limit_bytes=MIB),
        name="stack_parts",
    )(*[parts[j] for j in places])


def gradient_kernel(groups, marginals_ref, roots_ref, logs_ref, live_ref, tiles_ref, *refs):
    parts, (last_ref, *out_refs, table, grads, terms) = list(refs[: groups + 1]), refs[groups + 1 :]
    parts += [last_ref.at[j] for j in range(groups - 1)]
    far, chunk, width = parts[0].shape
    blocks, size = groups, grads.shape[0]
    here, core = lax.axis_index("chip"), lax.axis_index("core")
    z, near = lax.axis_index("far"), lax.axis_index("near")
    own = lax.rem(z * 2 + near, blocks)
    for other in range(2):
        for j in range(groups):
            block = jnp.bitwise_xor(here, j // 2) * 2 + jnp.bitwise_xor(core, other)
            for i in range(far):
                row = jnp.bitwise_xor(z, i) * 2 + jnp.bitwise_xor(near, j % 2)
                rows = pl.ds(pl.multiple_of(block * size + row * chunk, chunk), chunk)
                table[rows] = parts[other * groups + j][i].astype(table.dtype)

    marginals = marginals_ref[...].astype(jnp.float32)
    log_marg = jnp.log(marginals)
    log_total = jnp.log(jnp.sum(marginals, keepdims=True))
    own_rows = pl.ds(pl.multiple_of(own * size, size), size)
    own_vectors = table[own_rows].astype(jnp.bfloat16)
    own_log = jnp.log(marginals_ref[pl.ds(own, 1), :].astype(jnp.float32)) - log_total
    log_rows = jnp.transpose(jnp.broadcast_to(own_log, (128, size)))
    step = 64
    for v in range(blocks):
        vectors = table[v * size : (v + 1) * size].astype(jnp.bfloat16)
        visited = LOSS_SCALE * tiles_ref[v : v + 1]
        for first in range(0, size, step):
            rows = slice(first, first + step)
            logits = lax.dot_general(own_vectors[rows], vectors, NT, preferred_element_type=jnp.float32)
            log_row = jnp.concatenate([log_rows[rows]] * (size // 128), axis=1)
            margin = logits + log_row + log_marg[v : v + 1]
            live = live_ref[v, rows].astype(jnp.float32)
            weight = (0.25 * LOSS_SCALE) * roots_ref[v, rows] + (0.1 * LOSS_SCALE) * live
            zeros = visited - LOSS_SCALE * live
            grad = weight * margin - (0.25 * LOSS_SCALE) * logs_ref[v, rows] + zeros * jax.nn.sigmoid(margin)
            grads[rows, v * size : (v + 1) * size] = grad.astype(jnp.bfloat16)
    terms[...] = lax.dot_general(grads[...], own_vectors, TN, preferred_element_type=jnp.float32)
    terms[own_rows] += jnp.dot(
        grads[...], table[...].astype(jnp.bfloat16), preferred_element_type=jnp.float32
    )
    for j in range(blocks // 2):
        chip = jnp.bitwise_xor(here, j)
        first = 0
        for kept_ref, sent_ref in (out_refs[:2], out_refs[2:]):
            count = kept_ref.shape[1]
            stay = pl.multiple_of((2 * chip + core) * size + first, 16)
            leave = pl.multiple_of((2 * chip + 1 - core) * size + first, 16)
            kept_ref[j] = terms[pl.ds(stay, count)]
            sent_ref[j] = terms[pl.ds(leave, count)].astype(jnp.bfloat16)
            first += count


def swap(value, axis, bits):
    axes, bits = (axis, bits) if isinstance(axis, tuple) else ((axis,), (bits,))
    sizes = [lax.axis_size(name) for name in axes]
    both = 0
    for length, bit in zip(sizes, bits):
        both = both * length + bit
    return lax.ppermute(value, axes, [(i, i ^ both) for i in range(math.prod(sizes))])


def others(ask, count):
    order = sorted(range(1, count), key=lambda i: (-(i & -2), i))
    answers = {i: ask(i) for i in order}
    return [answers[i] for i in range(1, count)]


def tree_sum(values):
    while len(values) > 1:
        values = [one + two for one, two in zip(values[0::2], values[1::2])]
    return values[0]


def reduce_half(kept, sent, steps):
    bf16, f32 = jnp.bfloat16, jnp.float32
    total = kept + swap(sent, "core", 1).astype(f32)
    while total.shape[0] > 1:
        half = total.shape[0] // 2
        total = total[:half] + swap(total[half:].astype(bf16), "chip", half).astype(f32)
    total = total[0]
    for axis, bit in steps:
        mine = total.astype(bf16)
        total = mine.astype(f32) + swap(mine, axis, bit).astype(f32)
    return total


def local(table, marginals, visits, counts):
    chips, far = lax.axis_size("chip"), lax.axis_size("far")
    groups = blocks = 2 * chips
    size = counts.shape[3]
    width = table.shape[2]
    bf16, f32 = jnp.bfloat16, jnp.float32

    sums = sum_counts(blocks, visits, counts[0, 0])
    piece = table[0]
    pieces = others(lambda i: swap(piece, "far", i), far)
    column = stack([piece.astype(bf16)] + pieces)
    parts = others(lambda j: swap(column, ("near", "chip"), (j % 2, j // 2)), groups)
    other_column = swap(column, "core", 1)
    other_column, *parts, sums = lax.optimization_barrier((other_column, *parts, sums))
    parts = [column] + parts + [other_column, swap(stack(parts), "core", 1)]

    heights = (size // 2, size // 2)
    halves = pl.pallas_call(
        functools.partial(gradient_kernel, groups),
        out_shape=[
            jax.ShapeDtypeStruct((chips, rows, width), dtype) for rows in heights for dtype in (f32, bf16)
        ],
        in_specs=[VMEM] * (7 + groups),
        out_specs=[VMEM] * 4,
        scratch_shapes=[
            pltpu.VMEM((blocks * size, width), f32 if column.shape[1] % 16 else bf16),
            pltpu.VMEM((size, blocks * size), bf16),
            pltpu.VMEM((blocks * size, width), f32),
        ],
        compiler_params=pltpu.CompilerParams(vmem_limit_bytes=(6 + 3 * blocks) * MIB),
        cost_estimate=pl.CostEstimate(
            flops=10 * blocks * size * size * width,
            bytes_accessed=12 * blocks * size * size,
            transcendentals=blocks * size * size,
        ),
        name="swivel_gradient",
    )(marginals.reshape(blocks, size), *sums, *parts)

    steps = [("near", 1)] + [("far", 1 << i) for i in range(far.bit_length() - 1)]
    orders = (steps, steps[-1:] + steps[:-1])
    streams = [
        reduce_half(kept, sent, order) for kept, sent, order in zip(halves[0::2], halves[1::2], orders)
    ]
    return jnp.concatenate(streams, axis=0)[None]


def solution(mesh):
    rows, cols = mesh.shape["row"], mesh.shape["col"]
    split = Mesh(mesh.devices.reshape(rows // 2, 2, cols // 2, 2), ROW + COL)
    return jax.shard_map(
        local,
        mesh=split,
        in_specs=(
            P(COL, ROW, None),
            P(),
            P(ROW, COL, None),
            P(ROW, COL, None, None, None),
        ),
        out_specs=P(COL, None, None),
        check_vma=False,
    )
```

```python
import functools
import math

import jax
import jax.numpy as jnp
from jax import lax
from jax.experimental import pallas as pl
from jax.experimental.pallas import tpu as pltpu
from jax.sharding import Mesh, PartitionSpec as P

LOSS_SCALE = 0.0625
ROW = ("far", "near")
COL = ("chip", "core")
NT = (((1,), (1,)), ((), ()))
TN = (((0,), (0,)), ((), ()))
VMEM = pl.BlockSpec(memory_space=pltpu.VMEM)


MIB = 1024 * 1024


def count_kernel(tiles, visits_ref, counts_ref, roots_ref, logs_ref, live_ref, tiles_ref, visits, held, visits_sem, sems):
    size = counts_ref.shape[1]
    step = 32

    def fetch(k):
        return pltpu.make_async_copy(counts_ref.at[k], held.at[k], sems.at[k])

    fetch_visits = pltpu.make_async_copy(visits_ref, visits, visits_sem)
    fetch_visits.start()
    for k in range(tiles):
        fetch(k).start()
    for ref in (roots_ref, logs_ref, live_ref):
        ref[...] = jnp.zeros_like(ref)
    fetch_visits.wait()
    for v in range(tiles_ref.shape[0]):
        visited = 0
        for k in range(tiles):
            visited += (visits[0, 0, k] == v).astype(jnp.int32)
        tiles_ref[v : v + 1] = jnp.full((1, tiles_ref.shape[1]), visited.astype(jnp.float32))

    def add_tile(k, carry):
        fetch(k).wait()
        v = visits[0, 0, k]
        for first in range(0, size, step):
            rows = pl.ds(first, step)
            n = held[k, rows].astype(jnp.float32)
            clipped = jnp.maximum(n, 1.0)
            root = n * lax.rsqrt(clipped)
            roots_ref[v, rows] += root
            logs_ref[v, rows] += (root + 0.4) * jnp.log(clipped)
            live_ref[v, rows] += jnp.minimum(n, 1.0).astype(jnp.bfloat16)
        return carry

    lax.fori_loop(0, tiles, add_tile, 0)


def sum_counts(blocks, visits, counts):
    tiles, size = counts.shape[:2]
    hbm = pl.BlockSpec(memory_space=pltpu.HBM)
    return pl.pallas_call(
        functools.partial(count_kernel, tiles),
        out_shape=[
            jax.ShapeDtypeStruct((blocks, size, size), jnp.float32),
            jax.ShapeDtypeStruct((blocks, size, size), jnp.float32),
            jax.ShapeDtypeStruct((blocks, size, size), jnp.bfloat16),
            jax.ShapeDtypeStruct((blocks, size), jnp.float32),
        ],
        in_specs=[hbm, hbm],
        out_specs=[VMEM] * 4,
        scratch_shapes=[
            pltpu.SMEM(visits.shape, jnp.int32),
            pltpu.VMEM(counts.shape, jnp.int32),
            pltpu.SemaphoreType.DMA,
            pltpu.SemaphoreType.DMA((tiles,)),
        ],
        compiler_params=pltpu.CompilerParams(vmem_limit_bytes=(12 + 2 * blocks) * MIB),
        cost_estimate=pl.CostEstimate(
            flops=10 * counts.size, bytes_accessed=4 * counts.size, transcendentals=2 * counts.size
        ),
        name="sum_counts",
    )(pltpu.with_memory_space_constraint(visits, pltpu.HBM), pltpu.with_memory_space_constraint(counts, pltpu.HBM))


def stack_kernel(places, *refs):
    *parts, out_ref = refs
    for j, part in zip(places, parts):
        out_ref[j] = part[...].astype(out_ref.dtype)


def stack(parts):
    places = [0, *range(2, len(parts)), 1]
    return pl.pallas_call(
        functools.partial(stack_kernel, places),
        out_shape=jax.ShapeDtypeStruct((len(parts), *parts[0].shape), jnp.bfloat16),
        in_specs=[VMEM] * len(parts),
        out_specs=VMEM,
        compiler_params=pltpu.CompilerParams(vmem_limit_bytes=MIB),
        name="stack_parts",
    )(*[parts[j] for j in places])


def gradient_kernel(groups, marginals_ref, roots_ref, logs_ref, live_ref, tiles_ref, *refs):
    parts, (last_ref, *out_refs, table, logits, grads, terms) = list(refs[: groups + 1]), refs[groups + 1 :]
    parts += [last_ref.at[j] for j in range(groups - 1)]
    far, chunk, width = parts[0].shape
    blocks, size = groups, grads.shape[0]
    here, core = lax.axis_index("chip"), lax.axis_index("core")
    z, near = lax.axis_index("far"), lax.axis_index("near")
    own = lax.rem(z * 2 + near, blocks)
    for other in range(2):
        for j in range(groups):
            block = jnp.bitwise_xor(here, j // 2) * 2 + jnp.bitwise_xor(core, other)
            for i in range(far):
                row = jnp.bitwise_xor(z, i) * 2 + jnp.bitwise_xor(near, j % 2)
                rows = pl.ds(pl.multiple_of(block * size + row * chunk, chunk), chunk)
                table[rows] = parts[other * groups + j][i].astype(table.dtype)

    marginals = marginals_ref[...].astype(jnp.float32)
    log_marg = jnp.log(marginals)
    log_total = jnp.log(jnp.sum(marginals, keepdims=True))
    own_rows = pl.ds(pl.multiple_of(own * size, size), size)
    own_vectors = table[own_rows].astype(jnp.bfloat16)
    own_log = jnp.log(marginals_ref[pl.ds(own, 1), :].astype(jnp.float32)) - log_total
    log_rows = jnp.transpose(jnp.broadcast_to(own_log, (128, size)))
    for v in range(blocks):
        vectors = table[v * size : (v + 1) * size].astype(jnp.bfloat16)
        logits[:, v * size : (v + 1) * size] = lax.dot_general(
            own_vectors, vectors, NT, preferred_element_type=jnp.float32
        )
    step = 64
    for v in range(blocks):
        visited = LOSS_SCALE * tiles_ref[v : v + 1]
        for first in range(0, size, step):
            rows = slice(first, first + step)
            log_row = jnp.concatenate([log_rows[rows]] * (size // 128), axis=1)
            margin = logits[rows, v * size : (v + 1) * size] + log_row + log_marg[v : v + 1]
            live = live_ref[v, rows].astype(jnp.float32)
            weight = (0.25 * LOSS_SCALE) * roots_ref[v, rows] + (0.1 * LOSS_SCALE) * live
            zeros = visited - LOSS_SCALE * live
            grad = weight * margin - (0.25 * LOSS_SCALE) * logs_ref[v, rows] + zeros * jax.nn.sigmoid(margin)
            grads[rows, v * size : (v + 1) * size] = grad.astype(jnp.bfloat16)
    terms[...] = lax.dot_general(grads[...], own_vectors, TN, preferred_element_type=jnp.float32)
    terms[own_rows] += jnp.dot(
        grads[...], table[...].astype(jnp.bfloat16), preferred_element_type=jnp.float32
    )
    for j in range(blocks // 2):
        chip = jnp.bitwise_xor(here, j)
        first = 0
        for kept_ref, sent_ref in (out_refs[:2], out_refs[2:]):
            count = kept_ref.shape[1]
            stay = pl.multiple_of((2 * chip + core) * size + first, 16)
            leave = pl.multiple_of((2 * chip + 1 - core) * size + first, 16)
            kept_ref[j] = terms[pl.ds(stay, count)]
            sent_ref[j] = terms[pl.ds(leave, count)].astype(jnp.bfloat16)
            first += count


def swap(value, axis, bits):
    axes, bits = (axis, bits) if isinstance(axis, tuple) else ((axis,), (bits,))
    sizes = [lax.axis_size(name) for name in axes]
    both = 0
    for length, bit in zip(sizes, bits):
        both = both * length + bit
    return lax.ppermute(value, axes, [(i, i ^ both) for i in range(math.prod(sizes))])


def others(ask, count):
    order = sorted(range(1, count), key=lambda i: (-(i & -2), i))
    answers = {i: ask(i) for i in order}
    return [answers[i] for i in range(1, count)]


def tree_sum(values):
    while len(values) > 1:
        values = [one + two for one, two in zip(values[0::2], values[1::2])]
    return values[0]


def reduce_half(kept, sent, steps):
    bf16, f32 = jnp.bfloat16, jnp.float32
    total = kept + swap(sent, "core", 1).astype(f32)
    while total.shape[0] > 1:
        half = total.shape[0] // 2
        total = total[:half] + swap(total[half:].astype(bf16), "chip", half).astype(f32)
    total = total[0]
    for axis, bit in steps:
        mine = total.astype(bf16)
        total = mine.astype(f32) + swap(mine, axis, bit).astype(f32)
    return total


def local(table, marginals, visits, counts):
    chips, far = lax.axis_size("chip"), lax.axis_size("far")
    groups = blocks = 2 * chips
    size = counts.shape[3]
    width = table.shape[2]
    bf16, f32 = jnp.bfloat16, jnp.float32

    sums = sum_counts(blocks, visits, counts[0, 0])
    piece = table[0]
    pieces = others(lambda i: swap(piece, "far", i), far)
    column = stack([piece.astype(bf16)] + pieces)
    parts = others(lambda j: swap(column, ("near", "chip"), (j % 2, j // 2)), groups)
    other_column = swap(column, "core", 1)
    other_column, *parts, sums = lax.optimization_barrier((other_column, *parts, sums))
    parts = [column] + parts + [other_column, swap(stack(parts), "core", 1)]

    heights = (size // 2, size // 2)
    halves = pl.pallas_call(
        functools.partial(gradient_kernel, groups),
        out_shape=[
            jax.ShapeDtypeStruct((chips, rows, width), dtype) for rows in heights for dtype in (f32, bf16)
        ],
        in_specs=[VMEM] * (7 + groups),
        out_specs=[VMEM] * 4,
        scratch_shapes=[
            pltpu.VMEM((blocks * size, width), f32 if column.shape[1] % 16 else bf16),
            pltpu.VMEM((size, blocks * size), f32),
            pltpu.VMEM((size, blocks * size), bf16),
            pltpu.VMEM((blocks * size, width), f32),
        ],
        compiler_params=pltpu.CompilerParams(vmem_limit_bytes=(6 + 3 * blocks) * MIB),
        cost_estimate=pl.CostEstimate(
            flops=10 * blocks * size * size * width,
            bytes_accessed=12 * blocks * size * size,
            transcendentals=blocks * size * size,
        ),
        name="swivel_gradient",
    )(marginals.reshape(blocks, size), *sums, *parts)

    steps = [("near", 1)] + [("far", 1 << i) for i in range(far.bit_length() - 1)]
    orders = (steps, steps[-1:] + steps[:-1])
    streams = [
        reduce_half(kept, sent, order) for kept, sent, order in zip(halves[0::2], halves[1::2], orders)
    ]
    return jnp.concatenate(streams, axis=0)[None]


def solution(mesh):
    rows, cols = mesh.shape["row"], mesh.shape["col"]
    split = Mesh(mesh.devices.reshape(rows // 2, 2, cols // 2, 2), ROW + COL)
    return jax.shard_map(
        local,
        mesh=split,
        in_specs=(
            P(COL, ROW, None),
            P(),
            P(ROW, COL, None),
            P(ROW, COL, None, None, None),
        ),
        out_specs=P(COL, None, None),
        check_vma=False,
    )
```

```python
import functools
import math

import jax
import jax.numpy as jnp
from jax import lax
from jax.experimental import pallas as pl
from jax.experimental.pallas import tpu as pltpu
from jax.sharding import Mesh, PartitionSpec as P

LOSS_SCALE = 0.0625
ROW = ("far", "near")
COL = ("chip", "core")
NT = (((1,), (1,)), ((), ()))
TN = (((0,), (0,)), ((), ()))
VMEM = pl.BlockSpec(memory_space=pltpu.VMEM)


MIB = 1024 * 1024


def count_kernel(tiles, visits_ref, counts_ref, roots_ref, logs_ref, live_ref, tiles_ref, visits, held, visits_sem, sems):
    size = counts_ref.shape[1]
    step = 32

    def fetch(k):
        return pltpu.make_async_copy(counts_ref.at[k], held.at[k], sems.at[k])

    fetch_visits = pltpu.make_async_copy(visits_ref, visits, visits_sem)
    fetch_visits.start()
    for k in range(tiles):
        fetch(k).start()
    for ref in (roots_ref, logs_ref, live_ref):
        ref[...] = jnp.zeros_like(ref)
    fetch_visits.wait()
    for v in range(tiles_ref.shape[0]):
        visited = 0
        for k in range(tiles):
            visited += (visits[0, 0, k] == v).astype(jnp.int32)
        tiles_ref[v : v + 1] = jnp.full((1, tiles_ref.shape[1]), visited.astype(jnp.float32))

    def add_tile(k, carry):
        fetch(k).wait()
        v = visits[0, 0, k]
        for first in range(0, size, step):
            rows = pl.ds(first, step)
            n = held[k, rows].astype(jnp.float32)
            clipped = jnp.maximum(n, 1.0)
            root = n * lax.rsqrt(clipped)
            roots_ref[v, rows] += root
            logs_ref[v, rows] += (root + 0.4) * jnp.log(clipped)
            live_ref[v, rows] += jnp.minimum(n, 1.0).astype(jnp.bfloat16)
        return carry

    lax.fori_loop(0, tiles, add_tile, 0)


def sum_counts(blocks, visits, counts):
    tiles, size = counts.shape[:2]
    hbm = pl.BlockSpec(memory_space=pltpu.HBM)
    return pl.pallas_call(
        functools.partial(count_kernel, tiles),
        out_shape=[
            jax.ShapeDtypeStruct((blocks, size, size), jnp.float32),
            jax.ShapeDtypeStruct((blocks, size, size), jnp.float32),
            jax.ShapeDtypeStruct((blocks, size, size), jnp.bfloat16),
            jax.ShapeDtypeStruct((blocks, size), jnp.float32),
        ],
        in_specs=[hbm, hbm],
        out_specs=[VMEM] * 4,
        scratch_shapes=[
            pltpu.SMEM(visits.shape, jnp.int32),
            pltpu.VMEM(counts.shape, jnp.int32),
            pltpu.SemaphoreType.DMA,
            pltpu.SemaphoreType.DMA((tiles,)),
        ],
        compiler_params=pltpu.CompilerParams(vmem_limit_bytes=(12 + 2 * blocks) * MIB),
        cost_estimate=pl.CostEstimate(
            flops=10 * counts.size, bytes_accessed=4 * counts.size, transcendentals=2 * counts.size
        ),
        name="sum_counts",
    )(pltpu.with_memory_space_constraint(visits, pltpu.HBM), pltpu.with_memory_space_constraint(counts, pltpu.HBM))


def stack_kernel(places, *refs):
    *parts, out_ref = refs
    for j, part in zip(places, parts):
        out_ref[j] = part[...].astype(out_ref.dtype)


def stack(parts):
    places = [0, *range(2, len(parts)), 1]
    return pl.pallas_call(
        functools.partial(stack_kernel, places),
        out_shape=jax.ShapeDtypeStruct((len(parts), *parts[0].shape), jnp.bfloat16),
        in_specs=[VMEM] * len(parts),
        out_specs=VMEM,
        compiler_params=pltpu.CompilerParams(vmem_limit_bytes=MIB),
        name="stack_parts",
    )(*[parts[j] for j in places])


def gradient_kernel(groups, marginals_ref, roots_ref, logs_ref, live_ref, tiles_ref, *refs):
    parts, (last_ref, *out_refs, table, logits, grads, terms) = list(refs[: groups + 1]), refs[groups + 1 :]
    parts += [last_ref.at[j] for j in range(groups - 1)]
    far, chunk, width = parts[0].shape
    blocks, size = groups, grads.shape[0]
    here, core = lax.axis_index("chip"), lax.axis_index("core")
    z, near = lax.axis_index("far"), lax.axis_index("near")
    own = lax.rem(z * 2 + near, blocks)
    for other in range(2):
        for j in range(groups):
            block = jnp.bitwise_xor(here, j // 2) * 2 + jnp.bitwise_xor(core, other)
            for i in range(far):
                row = jnp.bitwise_xor(z, i) * 2 + jnp.bitwise_xor(near, j % 2)
                rows = pl.ds(pl.multiple_of(block * size + row * chunk, chunk), chunk)
                table[rows] = parts[other * groups + j][i].astype(table.dtype)

    marginals = marginals_ref[...].astype(jnp.float32)
    log_marg = jnp.log(marginals)
    log_total = jnp.log(jnp.sum(marginals, keepdims=True))
    own_rows = pl.ds(pl.multiple_of(own * size, size), size)
    own_vectors = table[own_rows].astype(jnp.bfloat16)
    own_log = jnp.log(marginals_ref[pl.ds(own, 1), :].astype(jnp.float32)) - log_total
    log_rows = jnp.transpose(jnp.broadcast_to(own_log, (128, size)))
    for v in range(blocks):
        vectors = table[v * size : (v + 1) * size].astype(jnp.bfloat16)
        logits[:, v * size : (v + 1) * size] = lax.dot_general(
            own_vectors, vectors, NT, preferred_element_type=jnp.float32
        )
    step = 64
    for v in range(blocks):
        visited = LOSS_SCALE * tiles_ref[v : v + 1]
        for first in range(0, size, step):
            rows = slice(first, first + step)
            log_row = jnp.concatenate([log_rows[rows]] * (size // 128), axis=1)
            margin = logits[rows, v * size : (v + 1) * size] + log_row + log_marg[v : v + 1]
            live = live_ref[v, rows].astype(jnp.float32)
            weight = (0.25 * LOSS_SCALE) * roots_ref[v, rows] + (0.1 * LOSS_SCALE) * live
            zeros = visited - LOSS_SCALE * live
            grad = weight * margin - (0.25 * LOSS_SCALE) * logs_ref[v, rows] + zeros * jax.nn.sigmoid(margin)
            grads[rows, v * size : (v + 1) * size] = grad.astype(jnp.bfloat16)
    terms[...] = lax.dot_general(grads[...], own_vectors, TN, preferred_element_type=jnp.float32)
    terms[own_rows] += jnp.dot(
        grads[...], table[...].astype(jnp.bfloat16), preferred_element_type=jnp.float32
    )
    kept_ref, *sent_refs = out_refs
    half = size // 2
    for j in range(groups):
        chip = jnp.bitwise_xor(here, j // 2)
        first = jnp.bitwise_xor(near, j % 2) * half
        stay = pl.multiple_of((2 * chip + core) * size + first, half)
        leave = pl.multiple_of((2 * chip + 1 - core) * size + first, half)
        kept_ref[j] = terms[pl.ds(stay, half)]
        sent_refs[j // 2][j % 2] = terms[pl.ds(leave, half)].astype(jnp.bfloat16)


def swap(value, axis, bits):
    axes, bits = (axis, bits) if isinstance(axis, tuple) else ((axis,), (bits,))
    sizes = [lax.axis_size(name) for name in axes]
    both = 0
    for length, bit in zip(sizes, bits):
        both = both * length + bit
    return lax.ppermute(value, axes, [(i, i ^ both) for i in range(math.prod(sizes))])


def others(ask, count):
    order = sorted(range(1, count), key=lambda i: (-(i & -2), i))
    answers = {i: ask(i) for i in order}
    return [answers[i] for i in range(1, count)]


def tree_sum(values):
    while len(values) > 1:
        values = [one + two for one, two in zip(values[0::2], values[1::2])]
    return values[0]


def local(table, marginals, visits, counts):
    chips, far = lax.axis_size("chip"), lax.axis_size("far")
    groups = blocks = 2 * chips
    size = counts.shape[3]
    width = table.shape[2]
    bf16, f32 = jnp.bfloat16, jnp.float32

    sums = sum_counts(blocks, visits, counts[0, 0])
    piece = table[0]
    pieces = others(lambda i: swap(piece, "far", i), far)
    column = stack([piece.astype(bf16)] + pieces)
    parts = others(lambda j: swap(column, ("near", "chip"), (j % 2, j // 2)), groups)
    other_column = swap(column, "core", 1)
    *parts, other_column, sums = lax.optimization_barrier((*parts[::-1], other_column, sums))
    parts = parts[::-1]
    parts = [column] + parts + [other_column, swap(stack(parts), "core", 1)]

    kept, *sent = pl.pallas_call(
        functools.partial(gradient_kernel, groups),
        out_shape=[jax.ShapeDtypeStruct((groups, size // 2, width), f32)]
        + [jax.ShapeDtypeStruct((2, size // 2, width), bf16)] * chips,
        in_specs=[VMEM] * (7 + groups),
        out_specs=[VMEM] * (1 + chips),
        scratch_shapes=[
            pltpu.VMEM((blocks * size, width), f32 if column.shape[1] % 16 else bf16),
            pltpu.VMEM((size, blocks * size), f32),
            pltpu.VMEM((size, blocks * size), bf16),
            pltpu.VMEM((blocks * size, width), f32),
        ],
        compiler_params=pltpu.CompilerParams(vmem_limit_bytes=(6 + 3 * blocks) * MIB),
        cost_estimate=pl.CostEstimate(
            flops=10 * blocks * size * size * width,
            bytes_accessed=12 * blocks * size * size,
            transcendentals=blocks * size * size,
        ),
        name="swivel_gradient",
    )(marginals.reshape(blocks, size), *sums, *parts)

    received = [swap(part, "core", 1) for part in reversed(sent)][::-1]
    terms = [kept[j] + received[j // 2][j % 2].astype(f32) for j in range(groups)]
    shares = others(lambda j: swap(terms[j].astype(bf16), ("near", "chip"), (j % 2, j // 2)), groups)
    total = terms[0]
    for share in shares:
        total += share.astype(f32)
    bit = 1
    while bit < far:
        mine = total.astype(bf16)
        total = mine.astype(f32) + swap(mine, "far", bit).astype(f32)
        bit *= 2
    mine = total.astype(bf16)
    other = swap(mine, "near", 1)
    first = lax.axis_index("near") == 0
    both = jnp.stack([jnp.where(first, mine, other), jnp.where(first, other, mine)])
    return both.reshape(1, size, width).astype(f32)


def solution(mesh):
    rows, cols = mesh.shape["row"], mesh.shape["col"]
    split = Mesh(mesh.devices.reshape(rows // 2, 2, cols // 2, 2), ROW + COL)
    return jax.shard_map(
        local,
        mesh=split,
        in_specs=(
            P(COL, ROW, None),
            P(),
            P(ROW, COL, None),
            P(ROW, COL, None, None, None),
        ),
        out_specs=P(COL, None, None),
        check_vma=False,
    )
```

```python
import functools
import math

import jax
import jax.numpy as jnp
from jax import lax
from jax.experimental import pallas as pl
from jax.experimental.pallas import tpu as pltpu
from jax.sharding import Mesh, PartitionSpec as P

LOSS_SCALE = 0.0625
ROW = ("far", "near")
COL = ("chip", "core")
NT = (((1,), (1,)), ((), ()))
TN = (((0,), (0,)), ((), ()))
VMEM = pl.BlockSpec(memory_space=pltpu.VMEM)


MIB = 1024 * 1024


def count_kernel(tiles, visits_ref, counts_ref, roots_ref, logs_ref, live_ref, tiles_ref, visits, held, visits_sem, sems):
    size = counts_ref.shape[1]
    step = 32

    def fetch(k):
        return pltpu.make_async_copy(counts_ref.at[k], held.at[k], sems.at[k])

    fetch_visits = pltpu.make_async_copy(visits_ref, visits, visits_sem)
    fetch_visits.start()
    for k in range(tiles):
        fetch(k).start()
    for ref in (roots_ref, logs_ref, live_ref):
        ref[...] = jnp.zeros_like(ref)
    fetch_visits.wait()
    for v in range(tiles_ref.shape[0]):
        visited = 0
        for k in range(tiles):
            visited += (visits[0, 0, k] == v).astype(jnp.int32)
        tiles_ref[v : v + 1] = jnp.full((1, tiles_ref.shape[1]), visited.astype(jnp.float32))

    def add_tile(k, carry):
        fetch(k).wait()
        v = visits[0, 0, k]
        for first in range(0, size, step):
            rows = pl.ds(first, step)
            n = held[k, rows].astype(jnp.float32)
            clipped = jnp.maximum(n, 1.0)
            root = n * lax.rsqrt(clipped)
            roots_ref[v, rows] += root
            logs_ref[v, rows] += (root + 0.4) * jnp.log(clipped)
            live_ref[v, rows] += jnp.minimum(n, 1.0).astype(jnp.bfloat16)
        return carry

    lax.fori_loop(0, tiles, add_tile, 0)


def sum_counts(blocks, visits, counts):
    tiles, size = counts.shape[:2]
    hbm = pl.BlockSpec(memory_space=pltpu.HBM)
    return pl.pallas_call(
        functools.partial(count_kernel, tiles),
        out_shape=[
            jax.ShapeDtypeStruct((blocks, size, size), jnp.float32),
            jax.ShapeDtypeStruct((blocks, size, size), jnp.float32),
            jax.ShapeDtypeStruct((blocks, size, size), jnp.bfloat16),
            jax.ShapeDtypeStruct((blocks, size), jnp.float32),
        ],
        in_specs=[hbm, hbm],
        out_specs=[VMEM] * 4,
        scratch_shapes=[
            pltpu.SMEM(visits.shape, jnp.int32),
            pltpu.VMEM(counts.shape, jnp.int32),
            pltpu.SemaphoreType.DMA,
            pltpu.SemaphoreType.DMA((tiles,)),
        ],
        compiler_params=pltpu.CompilerParams(vmem_limit_bytes=(12 + 2 * blocks) * MIB),
        cost_estimate=pl.CostEstimate(
            flops=10 * counts.size, bytes_accessed=4 * counts.size, transcendentals=2 * counts.size
        ),
        name="sum_counts",
    )(pltpu.with_memory_space_constraint(visits, pltpu.HBM), pltpu.with_memory_space_constraint(counts, pltpu.HBM))


def stack_kernel(places, *refs):
    *parts, out_ref = refs
    for j, part in zip(places, parts):
        out_ref[j] = part[...].astype(out_ref.dtype)


def stack(parts):
    places = [0, *range(2, len(parts)), 1]
    return pl.pallas_call(
        functools.partial(stack_kernel, places),
        out_shape=jax.ShapeDtypeStruct((len(parts), *parts[0].shape), jnp.bfloat16),
        in_specs=[VMEM] * len(parts),
        out_specs=VMEM,
        compiler_params=pltpu.CompilerParams(vmem_limit_bytes=MIB),
        name="stack_parts",
    )(*[parts[j] for j in places])


def gradient_kernel(groups, marginals_ref, roots_ref, logs_ref, live_ref, tiles_ref, *refs):
    parts, (last_ref, *out_refs, table, logits, grads, terms) = list(refs[: groups + 1]), refs[groups + 1 :]
    parts += [last_ref.at[j] for j in range(groups - 1)]
    far, chunk, width = parts[0].shape
    blocks, size = groups, grads.shape[0]
    here, core = lax.axis_index("chip"), lax.axis_index("core")
    z, near = lax.axis_index("far"), lax.axis_index("near")
    own = lax.rem(z * 2 + near, blocks)
    for other in range(2):
        for j in range(groups):
            block = jnp.bitwise_xor(here, j // 2) * 2 + jnp.bitwise_xor(core, other)
            for i in range(far):
                row = jnp.bitwise_xor(z, i) * 2 + jnp.bitwise_xor(near, j % 2)
                rows = pl.ds(pl.multiple_of(block * size + row * chunk, chunk), chunk)
                table[rows] = parts[other * groups + j][i].astype(table.dtype)

    marginals = marginals_ref[...].astype(jnp.float32)
    log_marg = jnp.log(marginals)
    log_total = jnp.log(jnp.sum(marginals, keepdims=True))
    own_rows = pl.ds(pl.multiple_of(own * size, size), size)
    own_vectors = table[own_rows].astype(jnp.bfloat16)
    own_log = jnp.log(marginals_ref[pl.ds(own, 1), :].astype(jnp.float32)) - log_total
    log_rows = jnp.transpose(jnp.broadcast_to(own_log, (128, size)))
    for v in range(blocks):
        vectors = table[v * size : (v + 1) * size].astype(jnp.bfloat16)
        logits[:, v * size : (v + 1) * size] = lax.dot_general(
            own_vectors, vectors, NT, preferred_element_type=jnp.float32
        )
    step = 64
    for v in range(blocks):
        visited = LOSS_SCALE * tiles_ref[v : v + 1]
        for first in range(0, size, step):
            rows = slice(first, first + step)
            log_row = jnp.concatenate([log_rows[rows]] * (size // 128), axis=1)
            margin = logits[rows, v * size : (v + 1) * size] + log_row + log_marg[v : v + 1]
            live = live_ref[v, rows].astype(jnp.float32)
            weight = (0.25 * LOSS_SCALE) * roots_ref[v, rows] + (0.1 * LOSS_SCALE) * live
            zeros = visited - LOSS_SCALE * live
            grad = weight * margin - (0.25 * LOSS_SCALE) * logs_ref[v, rows] + zeros * jax.nn.sigmoid(margin)
            grads[rows, v * size : (v + 1) * size] = grad.astype(jnp.bfloat16)
    terms[...] = lax.dot_general(grads[...], own_vectors, TN, preferred_element_type=jnp.float32)
    terms[own_rows] += jnp.dot(
        grads[...], table[...].astype(jnp.bfloat16), preferred_element_type=jnp.float32
    )
    for j in range(blocks // 2):
        chip = jnp.bitwise_xor(here, j)
        first = 0
        for kept_ref, sent_ref in (out_refs[:2], out_refs[2:]):
            count = kept_ref.shape[1]
            stay = pl.multiple_of((2 * chip + core) * size + first, 16)
            leave = pl.multiple_of((2 * chip + 1 - core) * size + first, 16)
            kept_ref[j] = terms[pl.ds(stay, count)]
            sent_ref[j] = terms[pl.ds(leave, count)].astype(jnp.bfloat16)
            first += count


def swap(value, axis, bits):
    axes, bits = (axis, bits) if isinstance(axis, tuple) else ((axis,), (bits,))
    sizes = [lax.axis_size(name) for name in axes]
    both = 0
    for length, bit in zip(sizes, bits):
        both = both * length + bit
    return lax.ppermute(value, axes, [(i, i ^ both) for i in range(math.prod(sizes))])


def others(ask, count):
    order = sorted(range(1, count), key=lambda i: (-(i & -2), i))
    answers = {i: ask(i) for i in order}
    return [answers[i] for i in range(1, count)]


def tree_sum(values):
    while len(values) > 1:
        values = [one + two for one, two in zip(values[0::2], values[1::2])]
    return values[0]


def reduce_half(kept, sent, steps):
    bf16, f32 = jnp.bfloat16, jnp.float32
    total = kept + swap(sent, "core", 1).astype(f32)
    while total.shape[0] > 1:
        half = total.shape[0] // 2
        total = total[:half] + swap(total[half:].astype(bf16), "chip", half).astype(f32)
    total = total[0]
    for axis, bit in steps:
        mine = total.astype(bf16)
        total = mine.astype(f32) + swap(mine, axis, bit).astype(f32)
    return total


def local(table, marginals, visits, counts):
    chips, far = lax.axis_size("chip"), lax.axis_size("far")
    groups = blocks = 2 * chips
    size = counts.shape[3]
    width = table.shape[2]
    bf16, f32 = jnp.bfloat16, jnp.float32

    sums = sum_counts(blocks, visits, counts[0, 0])
    piece = table[0]
    pieces = others(lambda i: swap(piece, "far", i), far)
    column = stack([piece.astype(bf16)] + pieces)
    parts = others(lambda j: swap(column, ("near", "chip"), (j % 2, j // 2)), groups)
    other_column = swap(column, "core", 1)
    *parts, other_column, sums = lax.optimization_barrier((*parts, other_column, sums))
    parts = [column] + parts + [other_column, swap(stack(parts), "core", 1)]

    heights = (size // 2, size // 2)
    halves = pl.pallas_call(
        functools.partial(gradient_kernel, groups),
        out_shape=[
            jax.ShapeDtypeStruct((chips, rows, width), dtype) for rows in heights for dtype in (f32, bf16)
        ],
        in_specs=[VMEM] * (7 + groups),
        out_specs=[VMEM] * 4,
        scratch_shapes=[
            pltpu.VMEM((blocks * size, width), f32 if column.shape[1] % 16 else bf16),
            pltpu.VMEM((size, blocks * size), f32),
            pltpu.VMEM((size, blocks * size), bf16),
            pltpu.VMEM((blocks * size, width), f32),
        ],
        compiler_params=pltpu.CompilerParams(vmem_limit_bytes=(6 + 3 * blocks) * MIB),
        cost_estimate=pl.CostEstimate(
            flops=10 * blocks * size * size * width,
            bytes_accessed=12 * blocks * size * size,
            transcendentals=blocks * size * size,
        ),
        name="swivel_gradient",
    )(marginals.reshape(blocks, size), *sums, *parts)

    steps = [("near", 1)] + [("far", 1 << i) for i in range(far.bit_length() - 1)]
    orders = (steps, steps[-1:] + steps[:-1])
    streams = [
        reduce_half(kept, sent, order) for kept, sent, order in zip(halves[0::2], halves[1::2], orders)
    ]
    return jnp.concatenate(streams, axis=0)[None]


def solution(mesh):
    rows, cols = mesh.shape["row"], mesh.shape["col"]
    split = Mesh(mesh.devices.reshape(rows // 2, 2, cols // 2, 2), ROW + COL)
    return jax.shard_map(
        local,
        mesh=split,
        in_specs=(
            P(COL, ROW, None),
            P(),
            P(ROW, COL, None),
            P(ROW, COL, None, None, None),
        ),
        out_specs=P(COL, None, None),
        check_vma=False,
    )
```

```python
import functools
import math

import jax
import jax.numpy as jnp
from jax import lax
from jax.experimental import pallas as pl
from jax.experimental.pallas import tpu as pltpu
from jax.sharding import Mesh, PartitionSpec as P

LOSS_SCALE = 0.0625
ROW = ("far", "near")
COL = ("chip", "core")
NT = (((1,), (1,)), ((), ()))
TN = (((0,), (0,)), ((), ()))
VMEM = pl.BlockSpec(memory_space=pltpu.VMEM)


MIB = 1024 * 1024


def count_kernel(tiles, visits_ref, counts_ref, roots_ref, logs_ref, live_ref, tiles_ref, visits, held, visits_sem, sems):
    size = counts_ref.shape[1]
    step = 32

    def fetch(k):
        return pltpu.make_async_copy(counts_ref.at[k], held.at[k], sems.at[k])

    fetch_visits = pltpu.make_async_copy(visits_ref, visits, visits_sem)
    fetch_visits.start()
    for k in range(tiles):
        fetch(k).start()
    for ref in (roots_ref, logs_ref, live_ref):
        ref[...] = jnp.zeros_like(ref)
    fetch_visits.wait()
    for v in range(tiles_ref.shape[0]):
        visited = 0
        for k in range(tiles):
            visited += (visits[0, 0, k] == v).astype(jnp.int32)
        tiles_ref[v : v + 1] = jnp.full((1, tiles_ref.shape[1]), visited.astype(jnp.float32))

    def add_tile(k, carry):
        fetch(k).wait()
        v = visits[0, 0, k]
        for first in range(0, size, step):
            rows = pl.ds(first, step)
            n = held[k, rows].astype(jnp.float32)
            clipped = jnp.maximum(n, 1.0)
            root = n * lax.rsqrt(clipped)
            roots_ref[v, rows] += root
            logs_ref[v, rows] += (root + 0.4) * jnp.log(clipped)
            live_ref[v, rows] += jnp.minimum(n, 1.0).astype(jnp.bfloat16)
        return carry

    lax.fori_loop(0, tiles, add_tile, 0)


def sum_counts(blocks, visits, counts):
    tiles, size = counts.shape[:2]
    hbm = pl.BlockSpec(memory_space=pltpu.HBM)
    return pl.pallas_call(
        functools.partial(count_kernel, tiles),
        out_shape=[
            jax.ShapeDtypeStruct((blocks, size, size), jnp.float32),
            jax.ShapeDtypeStruct((blocks, size, size), jnp.float32),
            jax.ShapeDtypeStruct((blocks, size, size), jnp.bfloat16),
            jax.ShapeDtypeStruct((blocks, size), jnp.float32),
        ],
        in_specs=[hbm, hbm],
        out_specs=[VMEM] * 4,
        scratch_shapes=[
            pltpu.SMEM(visits.shape, jnp.int32),
            pltpu.VMEM(counts.shape, jnp.int32),
            pltpu.SemaphoreType.DMA,
            pltpu.SemaphoreType.DMA((tiles,)),
        ],
        compiler_params=pltpu.CompilerParams(vmem_limit_bytes=(12 + 2 * blocks) * MIB),
        cost_estimate=pl.CostEstimate(
            flops=10 * counts.size, bytes_accessed=4 * counts.size, transcendentals=2 * counts.size
        ),
        name="sum_counts",
    )(pltpu.with_memory_space_constraint(visits, pltpu.HBM), pltpu.with_memory_space_constraint(counts, pltpu.HBM))


def stack_kernel(places, *refs):
    *parts, out_ref = refs
    for j, part in zip(places, parts):
        out_ref[j] = part[...].astype(out_ref.dtype)


def stack(parts):
    places = [0, *range(2, len(parts)), 1]
    return pl.pallas_call(
        functools.partial(stack_kernel, places),
        out_shape=jax.ShapeDtypeStruct((len(parts), *parts[0].shape), jnp.bfloat16),
        in_specs=[VMEM] * len(parts),
        out_specs=VMEM,
        compiler_params=pltpu.CompilerParams(vmem_limit_bytes=MIB),
        name="stack_parts",
    )(*[parts[j] for j in places])


def gradient_kernel(groups, marginals_ref, roots_ref, logs_ref, live_ref, tiles_ref, *refs):
    parts, (last_ref, *out_refs, table, logits, grads, terms) = list(refs[: groups + 1]), refs[groups + 1 :]
    parts += [last_ref.at[j] for j in range(groups - 1)]
    far, chunk, width = parts[0].shape
    blocks, size = groups, grads.shape[0]
    here, core = lax.axis_index("chip"), lax.axis_index("core")
    z, near = lax.axis_index("far"), lax.axis_index("near")
    own = lax.rem(z * 2 + near, blocks)
    for other in range(2):
        for j in range(groups):
            block = jnp.bitwise_xor(here, j // 2) * 2 + jnp.bitwise_xor(core, other)
            for i in range(far):
                row = jnp.bitwise_xor(z, i) * 2 + jnp.bitwise_xor(near, j % 2)
                rows = pl.ds(pl.multiple_of(block * size + row * chunk, chunk), chunk)
                table[rows] = parts[other * groups + j][i].astype(table.dtype)

    marginals = marginals_ref[...].astype(jnp.float32)
    log_marg = jnp.log(marginals)
    log_total = jnp.log(jnp.sum(marginals, keepdims=True))
    own_rows = pl.ds(pl.multiple_of(own * size, size), size)
    own_vectors = table[own_rows].astype(jnp.bfloat16)
    own_log = jnp.log(marginals_ref[pl.ds(own, 1), :].astype(jnp.float32)) - log_total
    log_rows = jnp.transpose(jnp.broadcast_to(own_log, (128, size)))
    for v in range(blocks):
        vectors = table[v * size : (v + 1) * size].astype(jnp.bfloat16)
        logits[:, v * size : (v + 1) * size] = lax.dot_general(
            own_vectors, vectors, NT, preferred_element_type=jnp.float32
        )
    step = 64
    for v in range(blocks):
        visited = LOSS_SCALE * tiles_ref[v : v + 1]
        for first in range(0, size, step):
            rows = slice(first, first + step)
            log_row = jnp.concatenate([log_rows[rows]] * (size // 128), axis=1)
            margin = logits[rows, v * size : (v + 1) * size] + log_row + log_marg[v : v + 1]
            live = live_ref[v, rows].astype(jnp.float32)
            weight = (0.25 * LOSS_SCALE) * roots_ref[v, rows] + (0.1 * LOSS_SCALE) * live
            zeros = visited - LOSS_SCALE * live
            grad = weight * margin - (0.25 * LOSS_SCALE) * logs_ref[v, rows] + zeros * jax.nn.sigmoid(margin)
            grads[rows, v * size : (v + 1) * size] = grad.astype(jnp.bfloat16)
    terms[...] = lax.dot_general(grads[...], own_vectors, TN, preferred_element_type=jnp.float32)
    terms[own_rows] += jnp.dot(
        grads[...], table[...].astype(jnp.bfloat16), preferred_element_type=jnp.float32
    )
    for j in range(blocks // 2):
        chip = jnp.bitwise_xor(here, j)
        first = 0
        for kept_ref, sent_ref in (out_refs[:2], out_refs[2:]):
            count = kept_ref.shape[1]
            stay = pl.multiple_of((2 * chip + core) * size + first, 16)
            leave = pl.multiple_of((2 * chip + 1 - core) * size + first, 16)
            kept_ref[j] = terms[pl.ds(stay, count)]
            sent_ref[j] = terms[pl.ds(leave, count)].astype(jnp.bfloat16)
            first += count


def swap(value, axis, bits):
    axes, bits = (axis, bits) if isinstance(axis, tuple) else ((axis,), (bits,))
    sizes = [lax.axis_size(name) for name in axes]
    both = 0
    for length, bit in zip(sizes, bits):
        both = both * length + bit
    return lax.ppermute(value, axes, [(i, i ^ both) for i in range(math.prod(sizes))])


def others(ask, count):
    order = sorted(range(1, count), key=lambda i: (-(i & -2), i))
    answers = {i: ask(i) for i in order}
    return [answers[i] for i in range(1, count)]


def tree_sum(values):
    while len(values) > 1:
        values = [one + two for one, two in zip(values[0::2], values[1::2])]
    return values[0]


def reduce_half(kept, sent, steps):
    bf16, f32 = jnp.bfloat16, jnp.float32
    total = kept + swap(sent, "core", 1).astype(f32)
    while total.shape[0] > 1:
        half = total.shape[0] // 2
        total = total[:half] + swap(total[half:].astype(bf16), "chip", half).astype(f32)
    total = total[0]
    for axis, bit in steps:
        mine = total.astype(bf16)
        total = mine.astype(f32) + swap(mine, axis, bit).astype(f32)
    return total


def local(table, marginals, visits, counts):
    chips, far = lax.axis_size("chip"), lax.axis_size("far")
    groups = blocks = 2 * chips
    size = counts.shape[3]
    width = table.shape[2]
    bf16, f32 = jnp.bfloat16, jnp.float32

    sums = sum_counts(blocks, visits, counts[0, 0])
    piece = table[0]
    pieces = others(lambda i: swap(piece, "far", i), far)
    column = stack([piece.astype(bf16)] + pieces)
    parts = others(lambda j: swap(column, ("near", "chip"), (j % 2, j // 2)), groups)
    other_column = swap(column, "core", 1)
    other_column, *parts, sums = lax.optimization_barrier((other_column, *parts, sums))
    parts = [column] + parts + [other_column, swap(stack(parts), "core", 1)]

    heights = (size // 2, size // 2)
    halves = pl.pallas_call(
        functools.partial(gradient_kernel, groups),
        out_shape=[
            jax.ShapeDtypeStruct((chips, rows, width), dtype) for rows in heights for dtype in (f32, bf16)
        ],
        in_specs=[VMEM] * (7 + groups),
        out_specs=[VMEM] * 4,
        scratch_shapes=[
            pltpu.VMEM((blocks * size, width), f32 if column.shape[1] % 16 else bf16),
            pltpu.VMEM((size, blocks * size), f32),
            pltpu.VMEM((size, blocks * size), bf16),
            pltpu.VMEM((blocks * size, width), f32),
        ],
        compiler_params=pltpu.CompilerParams(vmem_limit_bytes=(6 + 3 * blocks) * MIB),
        cost_estimate=pl.CostEstimate(
            flops=10 * blocks * size * size * width,
            bytes_accessed=12 * blocks * size * size,
            transcendentals=blocks * size * size,
        ),
        name="swivel_gradient",
    )(marginals.reshape(blocks, size), *sums, *parts)

    steps = [("near", 1)] + [("far", 1 << i) for i in range(far.bit_length() - 1)]
    orders = (steps, steps[-1:] + steps[:-1])
    streams = [
        reduce_half(kept, sent, order) for kept, sent, order in zip(halves[0::2], halves[1::2], orders)
    ]
    first, second = streams
    result = lax.optimization_barrier(jnp.pad(first, ((0, second.shape[0]), (0, 0)))[None])
    return lax.dynamic_update_slice(result, second[None], (0, first.shape[0], 0))


def solution(mesh):
    rows, cols = mesh.shape["row"], mesh.shape["col"]
    split = Mesh(mesh.devices.reshape(rows // 2, 2, cols // 2, 2), ROW + COL)
    return jax.shard_map(
        local,
        mesh=split,
        in_specs=(
            P(COL, ROW, None),
            P(),
            P(ROW, COL, None),
            P(ROW, COL, None, None, None),
        ),
        out_specs=P(COL, None, None),
        check_vma=False,
    )
```

```python
import functools
import math

import jax
import jax.numpy as jnp
from jax import lax
from jax.experimental import pallas as pl
from jax.experimental.pallas import tpu as pltpu
from jax.sharding import Mesh, PartitionSpec as P

LOSS_SCALE = 0.0625
ROW = ("far", "near")
COL = ("chip", "core")
NT = (((1,), (1,)), ((), ()))
TN = (((0,), (0,)), ((), ()))
VMEM = pl.BlockSpec(memory_space=pltpu.VMEM)


MIB = 1024 * 1024


def count_kernel(tiles, visits_ref, counts_ref, roots_ref, logs_ref, live_ref, tiles_ref, visits, held, visits_sem, sems):
    size = counts_ref.shape[1]
    step = 32

    def fetch(k):
        return pltpu.make_async_copy(counts_ref.at[k], held.at[k], sems.at[k])

    fetch_visits = pltpu.make_async_copy(visits_ref, visits, visits_sem)
    fetch_visits.start()
    for k in range(tiles):
        fetch(k).start()
    for ref in (roots_ref, logs_ref, live_ref):
        ref[...] = jnp.zeros_like(ref)
    fetch_visits.wait()
    for v in range(tiles_ref.shape[0]):
        visited = 0
        for k in range(tiles):
            visited += (visits[0, 0, k] == v).astype(jnp.int32)
        tiles_ref[v : v + 1] = jnp.full((1, tiles_ref.shape[1]), visited.astype(jnp.float32))

    def add_tile(k, carry):
        fetch(k).wait()
        v = visits[0, 0, k]
        for first in range(0, size, step):
            rows = pl.ds(first, step)
            n = held[k, rows].astype(jnp.float32)
            clipped = jnp.maximum(n, 1.0)
            root = n * lax.rsqrt(clipped)
            roots_ref[v, rows] += root
            logs_ref[v, rows] += (root + 0.4) * jnp.log(clipped)
            live_ref[v, rows] += jnp.minimum(n, 1.0).astype(jnp.bfloat16)
        return carry

    lax.fori_loop(0, tiles, add_tile, 0)


def sum_counts(blocks, visits, counts):
    tiles, size = counts.shape[:2]
    hbm = pl.BlockSpec(memory_space=pltpu.HBM)
    return pl.pallas_call(
        functools.partial(count_kernel, tiles),
        out_shape=[
            jax.ShapeDtypeStruct((blocks, size, size), jnp.float32),
            jax.ShapeDtypeStruct((blocks, size, size), jnp.float32),
            jax.ShapeDtypeStruct((blocks, size, size), jnp.bfloat16),
            jax.ShapeDtypeStruct((blocks, size), jnp.float32),
        ],
        in_specs=[hbm, hbm],
        out_specs=[VMEM] * 4,
        scratch_shapes=[
            pltpu.SMEM(visits.shape, jnp.int32),
            pltpu.VMEM(counts.shape, jnp.int32),
            pltpu.SemaphoreType.DMA,
            pltpu.SemaphoreType.DMA((tiles,)),
        ],
        compiler_params=pltpu.CompilerParams(vmem_limit_bytes=(12 + 2 * blocks) * MIB),
        cost_estimate=pl.CostEstimate(
            flops=10 * counts.size, bytes_accessed=4 * counts.size, transcendentals=2 * counts.size
        ),
        name="sum_counts",
    )(pltpu.with_memory_space_constraint(visits, pltpu.HBM), pltpu.with_memory_space_constraint(counts, pltpu.HBM))


def stack_kernel(places, *refs):
    *parts, out_ref = refs
    for j, part in zip(places, parts):
        out_ref[j] = part[...].astype(out_ref.dtype)


def stack(parts):
    places = [0, *range(2, len(parts)), 1]
    return pl.pallas_call(
        functools.partial(stack_kernel, places),
        out_shape=jax.ShapeDtypeStruct((len(parts), *parts[0].shape), jnp.bfloat16),
        in_specs=[VMEM] * len(parts),
        out_specs=VMEM,
        compiler_params=pltpu.CompilerParams(vmem_limit_bytes=MIB),
        name="stack_parts",
    )(*[parts[j] for j in places])


def gradient_kernel(groups, marginals_ref, roots_ref, logs_ref, live_ref, tiles_ref, *refs):
    parts, (*others_refs, table, logits, grads, terms) = list(refs[:groups]), refs[groups:]
    (low_ref, high_ref), out_refs = others_refs[:2], others_refs[2:]
    parts += [ref.at[j] for ref in (low_ref, high_ref) for j in range(groups // 2)]
    far, chunk, width = parts[0].shape
    blocks, size = groups, grads.shape[0]
    here, core = lax.axis_index("chip"), lax.axis_index("core")
    z, near = lax.axis_index("far"), lax.axis_index("near")
    own = lax.rem(z * 2 + near, blocks)
    for other in range(2):
        for j in range(groups):
            block = jnp.bitwise_xor(here, j // 2) * 2 + jnp.bitwise_xor(core, other)
            for i in range(far):
                row = jnp.bitwise_xor(z, i) * 2 + jnp.bitwise_xor(near, j % 2)
                rows = pl.ds(pl.multiple_of(block * size + row * chunk, chunk), chunk)
                table[rows] = parts[other * groups + j][i].astype(table.dtype)

    marginals = marginals_ref[...].astype(jnp.float32)
    log_marg = jnp.log(marginals)
    log_total = jnp.log(jnp.sum(marginals, keepdims=True))
    own_rows = pl.ds(pl.multiple_of(own * size, size), size)
    own_vectors = table[own_rows].astype(jnp.bfloat16)
    own_log = jnp.log(marginals_ref[pl.ds(own, 1), :].astype(jnp.float32)) - log_total
    log_rows = jnp.transpose(jnp.broadcast_to(own_log, (128, size)))
    for v in range(blocks):
        vectors = table[v * size : (v + 1) * size].astype(jnp.bfloat16)
        logits[:, v * size : (v + 1) * size] = lax.dot_general(
            own_vectors, vectors, NT, preferred_element_type=jnp.float32
        )
    step = 64
    for v in range(blocks):
        visited = LOSS_SCALE * tiles_ref[v : v + 1]
        for first in range(0, size, step):
            rows = slice(first, first + step)
            log_row = jnp.concatenate([log_rows[rows]] * (size // 128), axis=1)
            margin = logits[rows, v * size : (v + 1) * size] + log_row + log_marg[v : v + 1]
            live = live_ref[v, rows].astype(jnp.float32)
            weight = (0.25 * LOSS_SCALE) * roots_ref[v, rows] + (0.1 * LOSS_SCALE) * live
            zeros = visited - LOSS_SCALE * live
            grad = weight * margin - (0.25 * LOSS_SCALE) * logs_ref[v, rows] + zeros * jax.nn.sigmoid(margin)
            grads[rows, v * size : (v + 1) * size] = grad.astype(jnp.bfloat16)
    terms[...] = lax.dot_general(grads[...], own_vectors, TN, preferred_element_type=jnp.float32)
    terms[own_rows] += jnp.dot(
        grads[...], table[...].astype(jnp.bfloat16), preferred_element_type=jnp.float32
    )
    for j in range(blocks // 2):
        chip = jnp.bitwise_xor(here, j)
        first = 0
        for kept_ref, sent_ref in (out_refs[:2], out_refs[2:]):
            count = kept_ref.shape[1]
            stay = pl.multiple_of((2 * chip + core) * size + first, 16)
            leave = pl.multiple_of((2 * chip + 1 - core) * size + first, 16)
            kept_ref[j] = terms[pl.ds(stay, count)]
            sent_ref[j] = terms[pl.ds(leave, count)].astype(jnp.bfloat16)
            first += count


def swap(value, axis, bits):
    axes, bits = (axis, bits) if isinstance(axis, tuple) else ((axis,), (bits,))
    sizes = [lax.axis_size(name) for name in axes]
    both = 0
    for length, bit in zip(sizes, bits):
        both = both * length + bit
    return lax.ppermute(value, axes, [(i, i ^ both) for i in range(math.prod(sizes))])


def others(ask, count):
    order = sorted(range(1, count), key=lambda i: (-(i & -2), i))
    answers = {i: ask(i) for i in order}
    return [answers[i] for i in range(1, count)]


def tree_sum(values):
    while len(values) > 1:
        values = [one + two for one, two in zip(values[0::2], values[1::2])]
    return values[0]


def reduce_half(kept, sent, steps):
    bf16, f32 = jnp.bfloat16, jnp.float32
    total = kept + swap(sent, "core", 1).astype(f32)
    while total.shape[0] > 1:
        half = total.shape[0] // 2
        total = total[:half] + swap(total[half:].astype(bf16), "chip", half).astype(f32)
    total = total[0]
    for axis, bit in steps:
        mine = total.astype(bf16)
        total = mine.astype(f32) + swap(mine, axis, bit).astype(f32)
    return total


def local(table, marginals, visits, counts):
    chips, far = lax.axis_size("chip"), lax.axis_size("far")
    groups = blocks = 2 * chips
    size = counts.shape[3]
    width = table.shape[2]
    bf16, f32 = jnp.bfloat16, jnp.float32

    sums = sum_counts(blocks, visits, counts[0, 0])
    piece = table[0]
    pieces = others(lambda i: swap(piece, "far", i), far)
    column = stack([piece.astype(bf16)] + pieces)
    parts = others(lambda j: swap(column, ("near", "chip"), (j % 2, j // 2)), groups)
    *parts, sums = lax.optimization_barrier((*parts, sums))
    parts = [column] + parts
    parts += [swap(stack(some), "core", 1) for some in (parts[: groups // 2], parts[groups // 2 :])]

    heights = (size // 2, size // 2)
    halves = pl.pallas_call(
        functools.partial(gradient_kernel, groups),
        out_shape=[
            jax.ShapeDtypeStruct((chips, rows, width), dtype) for rows in heights for dtype in (f32, bf16)
        ],
        in_specs=[VMEM] * (7 + groups),
        out_specs=[VMEM] * 4,
        scratch_shapes=[
            pltpu.VMEM((blocks * size, width), f32 if column.shape[1] % 16 else bf16),
            pltpu.VMEM((size, blocks * size), f32),
            pltpu.VMEM((size, blocks * size), bf16),
            pltpu.VMEM((blocks * size, width), f32),
        ],
        compiler_params=pltpu.CompilerParams(vmem_limit_bytes=(6 + 3 * blocks) * MIB),
        cost_estimate=pl.CostEstimate(
            flops=10 * blocks * size * size * width,
            bytes_accessed=12 * blocks * size * size,
            transcendentals=blocks * size * size,
        ),
        name="swivel_gradient",
    )(marginals.reshape(blocks, size), *sums, *parts)

    steps = [("near", 1)] + [("far", 1 << i) for i in range(far.bit_length() - 1)]
    orders = (steps, steps[-1:] + steps[:-1])
    streams = [
        reduce_half(kept, sent, order) for kept, sent, order in zip(halves[0::2], halves[1::2], orders)
    ]
    first, second = streams
    result = lax.optimization_barrier(jnp.pad(first, ((0, second.shape[0]), (0, 0)))[None])
    return lax.dynamic_update_slice(result, second[None], (0, first.shape[0], 0))


def solution(mesh):
    rows, cols = mesh.shape["row"], mesh.shape["col"]
    split = Mesh(mesh.devices.reshape(rows // 2, 2, cols // 2, 2), ROW + COL)
    return jax.shard_map(
        local,
        mesh=split,
        in_specs=(
            P(COL, ROW, None),
            P(),
            P(ROW, COL, None),
            P(ROW, COL, None, None, None),
        ),
        out_specs=P(COL, None, None),
        check_vma=False,
    )
```

```python
import functools
import math

import jax
import jax.numpy as jnp
from jax import lax
from jax.experimental import pallas as pl
from jax.experimental.pallas import tpu as pltpu
from jax.sharding import Mesh, PartitionSpec as P

LOSS_SCALE = 0.0625
ROW = ("far", "near")
COL = ("chip", "core")
NT = (((1,), (1,)), ((), ()))
TN = (((0,), (0,)), ((), ()))
VMEM = pl.BlockSpec(memory_space=pltpu.VMEM)


MIB = 1024 * 1024


def count_kernel(tiles, visits_ref, counts_ref, roots_ref, logs_ref, live_ref, tiles_ref, visits, held, visits_sem, sems):
    size = counts_ref.shape[1]
    step = 32

    def fetch(k):
        return pltpu.make_async_copy(counts_ref.at[k], held.at[k], sems.at[k])

    fetch_visits = pltpu.make_async_copy(visits_ref, visits, visits_sem)
    fetch_visits.start()
    for k in range(tiles):
        fetch(k).start()
    for ref in (roots_ref, logs_ref, live_ref):
        ref[...] = jnp.zeros_like(ref)
    fetch_visits.wait()
    for v in range(tiles_ref.shape[0]):
        visited = 0
        for k in range(tiles):
            visited += (visits[0, 0, k] == v).astype(jnp.int32)
        tiles_ref[v : v + 1] = jnp.full((1, tiles_ref.shape[1]), visited.astype(jnp.float32))

    def add_tile(k, carry):
        fetch(k).wait()
        v = visits[0, 0, k]
        for first in range(0, size, step):
            rows = pl.ds(first, step)
            n = held[k, rows].astype(jnp.float32)
            clipped = jnp.maximum(n, 1.0)
            root = n * lax.rsqrt(clipped)
            roots_ref[v, rows] += root
            logs_ref[v, rows] += (root + 0.4) * jnp.log(clipped)
            live_ref[v, rows] += jnp.minimum(n, 1.0).astype(jnp.bfloat16)
        return carry

    lax.fori_loop(0, tiles, add_tile, 0)


def sum_counts(blocks, visits, counts):
    tiles, size = counts.shape[:2]
    hbm = pl.BlockSpec(memory_space=pltpu.HBM)
    return pl.pallas_call(
        functools.partial(count_kernel, tiles),
        out_shape=[
            jax.ShapeDtypeStruct((blocks, size, size), jnp.float32),
            jax.ShapeDtypeStruct((blocks, size, size), jnp.float32),
            jax.ShapeDtypeStruct((blocks, size, size), jnp.bfloat16),
            jax.ShapeDtypeStruct((blocks, size), jnp.float32),
        ],
        in_specs=[hbm, hbm],
        out_specs=[VMEM] * 4,
        scratch_shapes=[
            pltpu.SMEM(visits.shape, jnp.int32),
            pltpu.VMEM(counts.shape, jnp.int32),
            pltpu.SemaphoreType.DMA,
            pltpu.SemaphoreType.DMA((tiles,)),
        ],
        compiler_params=pltpu.CompilerParams(vmem_limit_bytes=(12 + 2 * blocks) * MIB),
        cost_estimate=pl.CostEstimate(
            flops=10 * counts.size, bytes_accessed=4 * counts.size, transcendentals=2 * counts.size
        ),
        name="sum_counts",
    )(pltpu.with_memory_space_constraint(visits, pltpu.HBM), pltpu.with_memory_space_constraint(counts, pltpu.HBM))


def stack_kernel(places, *refs):
    *parts, out_ref = refs
    for j, part in zip(places, parts):
        out_ref[j] = part[...].astype(out_ref.dtype)


def stack(parts):
    places = [0, *range(2, len(parts)), 1]
    return pl.pallas_call(
        functools.partial(stack_kernel, places),
        out_shape=jax.ShapeDtypeStruct((len(parts), *parts[0].shape), jnp.bfloat16),
        in_specs=[VMEM] * len(parts),
        out_specs=VMEM,
        compiler_params=pltpu.CompilerParams(vmem_limit_bytes=MIB),
        name="stack_parts",
    )(*[parts[j] for j in places])


def gradient_kernel(groups, marginals_ref, roots_ref, logs_ref, live_ref, tiles_ref, *refs):
    parts, (*others_refs, table, logits, grads, terms) = list(refs[:groups]), refs[groups:]
    (low_ref, high_ref), out_refs = others_refs[:2], others_refs[2:]
    parts += [ref.at[j] for ref in (low_ref, high_ref) for j in range(groups // 2)]
    far, chunk, width = parts[0].shape
    blocks, size = groups, grads.shape[0]
    here, core = lax.axis_index("chip"), lax.axis_index("core")
    z, near = lax.axis_index("far"), lax.axis_index("near")
    own = lax.rem(z * 2 + near, blocks)
    for other in range(2):
        for j in range(groups):
            block = jnp.bitwise_xor(here, j // 2) * 2 + jnp.bitwise_xor(core, other)
            for i in range(far):
                row = jnp.bitwise_xor(z, i) * 2 + jnp.bitwise_xor(near, j % 2)
                rows = pl.ds(pl.multiple_of(block * size + row * chunk, chunk), chunk)
                table[rows] = parts[other * groups + j][i].astype(table.dtype)

    marginals = marginals_ref[...].astype(jnp.float32)
    log_marg = jnp.log(marginals)
    log_total = jnp.log(jnp.sum(marginals, keepdims=True))
    own_rows = pl.ds(pl.multiple_of(own * size, size), size)
    own_vectors = table[own_rows].astype(jnp.bfloat16)
    own_log = jnp.log(marginals_ref[pl.ds(own, 1), :].astype(jnp.float32)) - log_total
    log_rows = jnp.transpose(jnp.broadcast_to(own_log, (128, size)))
    for v in range(blocks):
        vectors = table[v * size : (v + 1) * size].astype(jnp.bfloat16)
        logits[:, v * size : (v + 1) * size] = lax.dot_general(
            own_vectors, vectors, NT, preferred_element_type=jnp.float32
        )
    step = 32
    for v in range(blocks):
        visited = LOSS_SCALE * tiles_ref[v : v + 1]
        for first in range(0, size, step):
            rows = slice(first, first + step)
            log_row = jnp.concatenate([log_rows[rows]] * (size // 128), axis=1)
            margin = logits[rows, v * size : (v + 1) * size] + log_row + log_marg[v : v + 1]
            live = live_ref[v, rows].astype(jnp.float32)
            weight = (0.25 * LOSS_SCALE) * roots_ref[v, rows] + (0.1 * LOSS_SCALE) * live
            zeros = visited - LOSS_SCALE * live
            grad = weight * margin - (0.25 * LOSS_SCALE) * logs_ref[v, rows] + zeros * jax.nn.sigmoid(margin)
            grads[rows, v * size : (v + 1) * size] = grad.astype(jnp.bfloat16)
    terms[...] = lax.dot_general(grads[...], own_vectors, TN, preferred_element_type=jnp.float32)
    terms[own_rows] += jnp.dot(
        grads[...], table[...].astype(jnp.bfloat16), preferred_element_type=jnp.float32
    )
    for j in range(blocks // 2):
        chip = jnp.bitwise_xor(here, j)
        first = 0
        for kept_ref, sent_ref in (out_refs[:2], out_refs[2:]):
            count = kept_ref.shape[1]
            stay = pl.multiple_of((2 * chip + core) * size + first, 16)
            leave = pl.multiple_of((2 * chip + 1 - core) * size + first, 16)
            kept_ref[j] = terms[pl.ds(stay, count)]
            sent_ref[j] = terms[pl.ds(leave, count)].astype(jnp.bfloat16)
            first += count


def swap(value, axis, bits):
    axes, bits = (axis, bits) if isinstance(axis, tuple) else ((axis,), (bits,))
    sizes = [lax.axis_size(name) for name in axes]
    both = 0
    for length, bit in zip(sizes, bits):
        both = both * length + bit
    return lax.ppermute(value, axes, [(i, i ^ both) for i in range(math.prod(sizes))])


def others(ask, count):
    order = sorted(range(1, count), key=lambda i: (-(i & -2), i))
    answers = {i: ask(i) for i in order}
    return [answers[i] for i in range(1, count)]


def tree_sum(values):
    while len(values) > 1:
        values = [one + two for one, two in zip(values[0::2], values[1::2])]
    return values[0]


def reduce_half(kept, sent, steps):
    bf16, f32 = jnp.bfloat16, jnp.float32
    total = kept + swap(sent, "core", 1).astype(f32)
    while total.shape[0] > 1:
        half = total.shape[0] // 2
        total = total[:half] + swap(total[half:].astype(bf16), "chip", half).astype(f32)
    total = total[0]
    for axis, bit in steps:
        mine = total.astype(bf16)
        total = mine.astype(f32) + swap(mine, axis, bit).astype(f32)
    return total


def local(table, marginals, visits, counts):
    chips, far = lax.axis_size("chip"), lax.axis_size("far")
    groups = blocks = 2 * chips
    size = counts.shape[3]
    width = table.shape[2]
    bf16, f32 = jnp.bfloat16, jnp.float32

    sums = sum_counts(blocks, visits, counts[0, 0])
    piece = table[0]
    pieces = others(lambda i: swap(piece, "far", i), far)
    column = stack([piece.astype(bf16)] + pieces)
    parts = others(lambda j: swap(column, ("near", "chip"), (j % 2, j // 2)), groups)
    *parts, sums = lax.optimization_barrier((*parts, sums))
    parts = [column] + parts
    parts += [swap(stack(some), "core", 1) for some in (parts[: groups // 2], parts[groups // 2 :])]

    heights = (size // 2, size // 2)
    halves = pl.pallas_call(
        functools.partial(gradient_kernel, groups),
        out_shape=[
            jax.ShapeDtypeStruct((chips, rows, width), dtype) for rows in heights for dtype in (f32, bf16)
        ],
        in_specs=[VMEM] * (7 + groups),
        out_specs=[VMEM] * 4,
        scratch_shapes=[
            pltpu.VMEM((blocks * size, width), f32 if column.shape[1] % 16 else bf16),
            pltpu.VMEM((size, blocks * size), f32),
            pltpu.VMEM((size, blocks * size), bf16),
            pltpu.VMEM((blocks * size, width), f32),
        ],
        compiler_params=pltpu.CompilerParams(vmem_limit_bytes=(6 + 3 * blocks) * MIB),
        cost_estimate=pl.CostEstimate(
            flops=10 * blocks * size * size * width,
            bytes_accessed=12 * blocks * size * size,
            transcendentals=blocks * size * size,
        ),
        name="swivel_gradient",
    )(marginals.reshape(blocks, size), *sums, *parts)

    steps = [("near", 1)] + [("far", 1 << i) for i in range(far.bit_length() - 1)]
    orders = (steps, steps[-1:] + steps[:-1])
    streams = [
        reduce_half(kept, sent, order) for kept, sent, order in zip(halves[0::2], halves[1::2], orders)
    ]
    first, second = streams
    result = lax.optimization_barrier(jnp.pad(first, ((0, second.shape[0]), (0, 0)))[None])
    return lax.dynamic_update_slice(result, second[None], (0, first.shape[0], 0))


def solution(mesh):
    rows, cols = mesh.shape["row"], mesh.shape["col"]
    split = Mesh(mesh.devices.reshape(rows // 2, 2, cols // 2, 2), ROW + COL)
    return jax.shard_map(
        local,
        mesh=split,
        in_specs=(
            P(COL, ROW, None),
            P(),
            P(ROW, COL, None),
            P(ROW, COL, None, None, None),
        ),
        out_specs=P(COL, None, None),
        check_vma=False,
    )
```

```python
import functools
import math

import jax
import jax.numpy as jnp
from jax import lax
from jax.experimental import pallas as pl
from jax.experimental.pallas import tpu as pltpu
from jax.sharding import Mesh, PartitionSpec as P

LOSS_SCALE = 0.0625
ROW = ("far", "near")
COL = ("chip", "core")
NT = (((1,), (1,)), ((), ()))
TN = (((0,), (0,)), ((), ()))
VMEM = pl.BlockSpec(memory_space=pltpu.VMEM)


MIB = 1024 * 1024


def count_kernel(tiles, visits_ref, counts_ref, roots_ref, logs_ref, live_ref, tiles_ref, visits, held, visits_sem, sems):
    size = counts_ref.shape[1]
    step = 16

    def fetch(k):
        return pltpu.make_async_copy(counts_ref.at[k], held.at[k], sems.at[k])

    fetch_visits = pltpu.make_async_copy(visits_ref, visits, visits_sem)
    fetch_visits.start()
    for k in range(tiles):
        fetch(k).start()
    for ref in (roots_ref, logs_ref, live_ref):
        ref[...] = jnp.zeros_like(ref)
    fetch_visits.wait()
    for v in range(tiles_ref.shape[0]):
        visited = 0
        for k in range(tiles):
            visited += (visits[0, 0, k] == v).astype(jnp.int32)
        tiles_ref[v : v + 1] = jnp.full((1, tiles_ref.shape[1]), visited.astype(jnp.float32))

    def add_tile(k, carry):
        fetch(k).wait()
        v = visits[0, 0, k]
        for first in range(0, size, step):
            rows = pl.ds(first, step)
            n = held[k, rows].astype(jnp.float32)
            clipped = jnp.maximum(n, 1.0)
            root = n * lax.rsqrt(clipped)
            roots_ref[v, rows] += root
            logs_ref[v, rows] += (root + 0.4) * jnp.log(clipped)
            live_ref[v, rows] += jnp.minimum(n, 1.0).astype(jnp.bfloat16)
        return carry

    lax.fori_loop(0, tiles, add_tile, 0)


def sum_counts(blocks, visits, counts):
    tiles, size = counts.shape[:2]
    hbm = pl.BlockSpec(memory_space=pltpu.HBM)
    return pl.pallas_call(
        functools.partial(count_kernel, tiles),
        out_shape=[
            jax.ShapeDtypeStruct((blocks, size, size), jnp.float32),
            jax.ShapeDtypeStruct((blocks, size, size), jnp.float32),
            jax.ShapeDtypeStruct((blocks, size, size), jnp.bfloat16),
            jax.ShapeDtypeStruct((blocks, size), jnp.float32),
        ],
        in_specs=[hbm, hbm],
        out_specs=[VMEM] * 4,
        scratch_shapes=[
            pltpu.SMEM(visits.shape, jnp.int32),
            pltpu.VMEM(counts.shape, jnp.int32),
            pltpu.SemaphoreType.DMA,
            pltpu.SemaphoreType.DMA((tiles,)),
        ],
        compiler_params=pltpu.CompilerParams(vmem_limit_bytes=(12 + 2 * blocks) * MIB),
        cost_estimate=pl.CostEstimate(
            flops=10 * counts.size, bytes_accessed=4 * counts.size, transcendentals=2 * counts.size
        ),
        name="sum_counts",
    )(pltpu.with_memory_space_constraint(visits, pltpu.HBM), pltpu.with_memory_space_constraint(counts, pltpu.HBM))


def stack_kernel(places, *refs):
    *parts, out_ref = refs
    for j, part in zip(places, parts):
        out_ref[j] = part[...].astype(out_ref.dtype)


def stack(parts):
    places = [0, *range(2, len(parts)), 1]
    return pl.pallas_call(
        functools.partial(stack_kernel, places),
        out_shape=jax.ShapeDtypeStruct((len(parts), *parts[0].shape), jnp.bfloat16),
        in_specs=[VMEM] * len(parts),
        out_specs=VMEM,
        compiler_params=pltpu.CompilerParams(vmem_limit_bytes=MIB),
        name="stack_parts",
    )(*[parts[j] for j in places])


def gradient_kernel(groups, marginals_ref, roots_ref, logs_ref, live_ref, tiles_ref, *refs):
    parts, (*others_refs, table, logits, grads, terms) = list(refs[:groups]), refs[groups:]
    (low_ref, high_ref), out_refs = others_refs[:2], others_refs[2:]
    parts += [ref.at[j] for ref in (low_ref, high_ref) for j in range(groups // 2)]
    far, chunk, width = parts[0].shape
    blocks, size = groups, grads.shape[0]
    here, core = lax.axis_index("chip"), lax.axis_index("core")
    z, near = lax.axis_index("far"), lax.axis_index("near")
    own = lax.rem(z * 2 + near, blocks)
    for other in range(2):
        for j in range(groups):
            block = jnp.bitwise_xor(here, j // 2) * 2 + jnp.bitwise_xor(core, other)
            for i in range(far):
                row = jnp.bitwise_xor(z, i) * 2 + jnp.bitwise_xor(near, j % 2)
                rows = pl.ds(pl.multiple_of(block * size + row * chunk, chunk), chunk)
                table[rows] = parts[other * groups + j][i].astype(table.dtype)

    marginals = marginals_ref[...].astype(jnp.float32)
    log_marg = jnp.log(marginals)
    log_total = jnp.log(jnp.sum(marginals, keepdims=True))
    own_rows = pl.ds(pl.multiple_of(own * size, size), size)
    own_vectors = table[own_rows].astype(jnp.bfloat16)
    own_log = jnp.log(marginals_ref[pl.ds(own, 1), :].astype(jnp.float32)) - log_total
    log_rows = jnp.transpose(jnp.broadcast_to(own_log, (128, size)))
    for v in range(blocks):
        vectors = table[v * size : (v + 1) * size].astype(jnp.bfloat16)
        logits[:, v * size : (v + 1) * size] = lax.dot_general(
            own_vectors, vectors, NT, preferred_element_type=jnp.float32
        )
    step = 32
    for v in range(blocks):
        visited = LOSS_SCALE * tiles_ref[v : v + 1]
        for first in range(0, size, step):
            rows = slice(first, first + step)
            log_row = jnp.concatenate([log_rows[rows]] * (size // 128), axis=1)
            margin = logits[rows, v * size : (v + 1) * size] + log_row + log_marg[v : v + 1]
            live = live_ref[v, rows].astype(jnp.float32)
            weight = (0.25 * LOSS_SCALE) * roots_ref[v, rows] + (0.1 * LOSS_SCALE) * live
            zeros = visited - LOSS_SCALE * live
            grad = weight * margin - (0.25 * LOSS_SCALE) * logs_ref[v, rows] + zeros * jax.nn.sigmoid(margin)
            grads[rows, v * size : (v + 1) * size] = grad.astype(jnp.bfloat16)
    terms[...] = lax.dot_general(grads[...], own_vectors, TN, preferred_element_type=jnp.float32)
    terms[own_rows] += jnp.dot(
        grads[...], table[...].astype(jnp.bfloat16), preferred_element_type=jnp.float32
    )
    for j in range(blocks // 2):
        chip = jnp.bitwise_xor(here, j)
        first = 0
        for kept_ref, sent_ref in (out_refs[:2], out_refs[2:]):
            count = kept_ref.shape[1]
            stay = pl.multiple_of((2 * chip + core) * size + first, 16)
            leave = pl.multiple_of((2 * chip + 1 - core) * size + first, 16)
            kept_ref[j] = terms[pl.ds(stay, count)]
            sent_ref[j] = terms[pl.ds(leave, count)].astype(jnp.bfloat16)
            first += count


def swap(value, axis, bits):
    axes, bits = (axis, bits) if isinstance(axis, tuple) else ((axis,), (bits,))
    sizes = [lax.axis_size(name) for name in axes]
    both = 0
    for length, bit in zip(sizes, bits):
        both = both * length + bit
    return lax.ppermute(value, axes, [(i, i ^ both) for i in range(math.prod(sizes))])


def others(ask, count):
    order = sorted(range(1, count), key=lambda i: (-(i & -2), i))
    answers = {i: ask(i) for i in order}
    return [answers[i] for i in range(1, count)]


def tree_sum(values):
    while len(values) > 1:
        values = [one + two for one, two in zip(values[0::2], values[1::2])]
    return values[0]


def reduce_half(kept, sent, steps):
    bf16, f32 = jnp.bfloat16, jnp.float32
    total = kept + swap(sent, "core", 1).astype(f32)
    while total.shape[0] > 1:
        half = total.shape[0] // 2
        total = total[:half] + swap(total[half:].astype(bf16), "chip", half).astype(f32)
    total = total[0]
    for axis, bit in steps:
        mine = total.astype(bf16)
        total = mine.astype(f32) + swap(mine, axis, bit).astype(f32)
    return total


def local(table, marginals, visits, counts):
    chips, far = lax.axis_size("chip"), lax.axis_size("far")
    groups = blocks = 2 * chips
    size = counts.shape[3]
    width = table.shape[2]
    bf16, f32 = jnp.bfloat16, jnp.float32

    sums = sum_counts(blocks, visits, counts[0, 0])
    piece = table[0]
    pieces = others(lambda i: swap(piece, "far", i), far)
    column = stack([piece.astype(bf16)] + pieces)
    parts = others(lambda j: swap(column, ("near", "chip"), (j % 2, j // 2)), groups)
    *parts, sums = lax.optimization_barrier((*parts, sums))
    parts = [column] + parts
    parts += [swap(stack(some), "core", 1) for some in (parts[: groups // 2], parts[groups // 2 :])]

    heights = (size // 2, size // 2)
    halves = pl.pallas_call(
        functools.partial(gradient_kernel, groups),
        out_shape=[
            jax.ShapeDtypeStruct((chips, rows, width), dtype) for rows in heights for dtype in (f32, bf16)
        ],
        in_specs=[VMEM] * (7 + groups),
        out_specs=[VMEM] * 4,
        scratch_shapes=[
            pltpu.VMEM((blocks * size, width), f32 if column.shape[1] % 16 else bf16),
            pltpu.VMEM((size, blocks * size), f32),
            pltpu.VMEM((size, blocks * size), bf16),
            pltpu.VMEM((blocks * size, width), f32),
        ],
        compiler_params=pltpu.CompilerParams(vmem_limit_bytes=(6 + 3 * blocks) * MIB),
        cost_estimate=pl.CostEstimate(
            flops=10 * blocks * size * size * width,
            bytes_accessed=12 * blocks * size * size,
            transcendentals=blocks * size * size,
        ),
        name="swivel_gradient",
    )(marginals.reshape(blocks, size), *sums, *parts)

    steps = [("near", 1)] + [("far", 1 << i) for i in range(far.bit_length() - 1)]
    orders = (steps, steps[-1:] + steps[:-1])
    streams = [
        reduce_half(kept, sent, order) for kept, sent, order in zip(halves[0::2], halves[1::2], orders)
    ]
    first, second = streams
    result = lax.optimization_barrier(jnp.pad(first, ((0, second.shape[0]), (0, 0)))[None])
    return lax.dynamic_update_slice(result, second[None], (0, first.shape[0], 0))


def solution(mesh):
    rows, cols = mesh.shape["row"], mesh.shape["col"]
    split = Mesh(mesh.devices.reshape(rows // 2, 2, cols // 2, 2), ROW + COL)
    return jax.shard_map(
        local,
        mesh=split,
        in_specs=(
            P(COL, ROW, None),
            P(),
            P(ROW, COL, None),
            P(ROW, COL, None, None, None),
        ),
        out_specs=P(COL, None, None),
        check_vma=False,
    )
```
